256 devices in a mesh: row: 32 (over z, y), col: 8 (over x, core).
Axes of the slice: x: 4, y: 4, z: 8, core: 2. Of those that a mesh axis runs over, the one named last changes fastest.
Arguments:
- top_inverse: float32 [8192, 8192], P('row', 'col'), as said below
- panels: float32 [8192, 8192], P('row', 'col'), may hold values from -0.24 to 0.24
- fill_pattern: int32 [64, 64], P('col'), may hold values from 0 to 1, as said below
- diagonal_part: float32 [8192, 128], P('col'), as said below
Outputs:
- offdiag_inverse: float32 [8192, 8192], P('row', 'col')
- diagonal_inverse: float32 [8192, 128], P('col')
The draws below stay inside these ranges and needn't reach their ends.
Inputs may be any that keep to these rules, and one draw needn't show every extreme that they name: top_inverse is exactly symmetric. `fill_pattern`: every second-level supernode couples to at least one top block. Each 128 x 128 block of diagonal_part is exactly symmetric.
All inputs are finite; a program needn't handle non-finite values.
Results may differ from the reference program's by a relative error of at most 0.000075.
Values sent between devices are 32-bit elements; how exact they have to be, the bound alone decides.
A program may use at most 128 MiB of HBM per device.

```python
import math
import jax
import jax.numpy as jnp
from jax import lax

BLOCK = 128
TOP_BLOCKS = 64
CHILDREN = 64
ORDER = 8192


def draw_top_inverse(key, part):
    key = jax.random.fold_in(key, 1)
    key_one, key_two = jax.random.split(key, 2)
    random_entries = jax.random.normal(key_one, (ORDER, ORDER), jnp.float32)
    symmetric = (random_entries + random_entries.T) * (0.5 / math.sqrt(2.0 * ORDER))
    diagonal_base = jax.random.uniform(key_two, (ORDER,), jnp.float32, 1.0, 3.0)
    matrix = symmetric + jnp.diag(diagonal_base)
    return matrix


def draw_fill_pattern(key, part):
    key = jax.random.fold_in(key, 3)
    key_one, key_two, key_three = jax.random.split(key, 3)
    density = jax.random.randint(key_one, (CHILDREN, 1), 8, 57)
    random_draws = jax.random.randint(key_two, (CHILDREN, TOP_BLOCKS), 0, 64)
    parent = jax.random.randint(key_three, (CHILDREN, 1), 0, TOP_BLOCKS)
    column = jnp.arange(TOP_BLOCKS)[None, :]
    return jnp.where((random_draws < density) | (column == parent), 1, 0).astype(jnp.int32)


def draw_diagonal_part(key, part):
    key = jax.random.fold_in(key, 2)
    key_one, key_two = jax.random.split(key, 2)
    random_entries = jax.random.normal(key_one, (CHILDREN, BLOCK, BLOCK), jnp.float32)
    symmetric = (random_entries + jnp.swapaxes(random_entries, 1, 2)) * (0.5 / math.sqrt(2.0 * BLOCK))
    diagonal_base = jax.random.uniform(key_two, (CHILDREN, BLOCK, 1), jnp.float32, 1.0, 2.0) * jnp.eye(BLOCK, dtype=jnp.float32)[None]
    return (symmetric + diagonal_base).reshape(CHILDREN * BLOCK, BLOCK)


def block_scale(stream_key, extent, cuts, least, largest):
    def one(position, blocks):
        steps = jax.random.uniform(jax.random.fold_in(jax.random.fold_in(stream_key, 6), position), (blocks,), jnp.float32, least / len(cuts), largest / len(cuts))
        return jnp.repeat(jnp.exp(steps), extent[position] // blocks).reshape((-1,) + (1,) * (len(extent) - position - 1))

    level = one(*cuts[0])
    for cut in cuts[1:]:
        level = level * one(*cut)
    return level


def normal_values(stream_key, shape, spread, most, pieces=(), kind=jnp.bfloat16):
    factor_of = block_scale(stream_key, shape, pieces, -0.22, 0.18) if pieces else 1.0
    array = jax.random.normal(stream_key, shape, jnp.float32) * spread * factor_of
    return jnp.minimum(jnp.maximum(array, -most), most).astype(kind)


def setup_inputs(seed: int = 0) -> dict:
    keys = jax.random.split(jax.random.key(seed), 5)
    return {
        "top_inverse": draw_top_inverse(jax.random.fold_in(keys[4], 71), 0),
        "panels": normal_values(keys[1], (ORDER, CHILDREN * BLOCK), 0.04, 0.24, ((0, 32), (1, 8)), jnp.float32),
        "fill_pattern": draw_fill_pattern(jax.random.fold_in(keys[4], 71), 0),
        "diagonal_part": draw_diagonal_part(jax.random.fold_in(keys[4], 71), 0),
    }


def reference(top_inverse, panels, fill_pattern, diagonal_part):
    block_mask = jnp.repeat(jnp.repeat(fill_pattern.T.astype(jnp.float32), BLOCK, axis=0), BLOCK, axis=1)
    scaled_panel = panels * block_mask
    offdiag_inverse = -jnp.dot(top_inverse, scaled_panel, precision=lax.Precision.HIGHEST, preferred_element_type=jnp.float32) * block_mask
    diag_terms = jnp.einsum("mkb,mkc->kbc", scaled_panel.reshape(ORDER, CHILDREN, BLOCK), offdiag_inverse.reshape(ORDER, CHILDREN, BLOCK), precision=lax.Precision.HIGHEST)
    diagonal_inverse = diagonal_part - diag_terms.reshape(CHILDREN * BLOCK, BLOCK)
    return offdiag_inverse, diagonal_inverse
```

```python
import functools

import jax
import jax.numpy as jnp
from jax import lax
from jax.experimental import pallas as pl
from jax.experimental.pallas import tpu as pltpu
from jax.sharding import PartitionSpec as P

BLOCK = 128
Z, Y, X, CORES = 8, 4, 4, 2
ROWS = 2 * BLOCK
CHUNKS = 8
WAVES = ((0, 1), (2, 3), (4, 5), (6, 7))
GROUPS = 4
LINK = 90e3
HOP = 1.5


def steps(way, q):
    return 4 if q % 2 == way else 3


def zslot(way, s):
    return s if way == 0 else (Z - s) % Z


def arrival_of(q, d):
    if d < 4 or (d == 4 and q % 2 == 0):
        return ("z", 0, q, d - 1)
    return ("z", 1, q, Z - 1 - d)


class Plan:
    def __init__(self):
        self.tasks = []

    def add(self, name, rank, after=(), needs=(), sends=(), cost=0.0, gate=None):
        self.tasks.append(
            dict(name=name, rank=rank, after=after, needs=needs, sends=sends, cost=cost, gate=gate)
        )

    def order(self):
        now, free, arrived, done, result = 0.0, {}, {}, set(), []
        left = list(self.tasks)
        while left:
            best = None
            for task in left:
                if not all(n in done for n in task["after"]) or not all(n in arrived for n in task["needs"]):
                    continue
                ready = max([arrived[n] for n in task["needs"]], default=0.0)
                if task["gate"] is not None:
                    link, depth = task["gate"]
                    ready = max(ready, free.get(link, 0.0) - depth)
                ready = max(ready, now)
                key = (ready, task["rank"])
                if best is None or key < best[0]:
                    best = (key, task)
            (ready, _), task = best
            now = ready + task["cost"]
            for ident, link, size in task["sends"]:
                now += 0.05
                if link is None:
                    arrived[ident] = now + 2.5
                else:
                    rate = 6 * LINK if link == "s" else LINK
                    begin = max(now, free.get(link, 0.0))
                    free[link] = begin + size / rate
                    arrived[ident] = free[link] + HOP
            done.add(task["name"])
            left.remove(task)
            result.append((ready, task))
        return result, now


def make_plan():
    plan = Plan()
    piece = ROWS * BLOCK * 4 * CORES
    for q in range(CHUNKS):
        plan.add(("mask", q), (1, q) if q else (0, 0), cost=0.15)
        for way in range(2):
            plan.add(
                ("zown", way, q), (0, 1, way) if q == 0 else (2, q, way),
                after=[("mask", q)] + ([("zown", way, q - 1)] if q else []),
                sends=[(("z", way, q, 0), ("z", way), piece)], gate=(("z", way), 5.5),
            )
            for s in range(1, steps(way, q)):
                plan.add(
                    ("zfwd", way, q, s), (1, q, s), needs=[("z", way, q, s - 1)],
                    sends=[(("z", way, q, s), ("z", way), piece)],
                )
    block = ROWS * ROWS * 4 * CORES
    plan.add(
        ("a2a",), (0, 2),
        sends=[(("a", 3), ("y", 0), block), (("a", 1), ("y", 1), block), (("a", 2), ("y", 0), 2 * block)],
    )
    plan.add(("acopy",), (0, 3), cost=0.15)
    for j in range(Y):
        plan.add(
            ("xown", j), (0, 4), after=[("acopy",)], needs=[("a", j)] if j else [],
            sends=[(("x", 1, j), ("x", 0), block), (("x", 3, j), ("x", 1), block), (("s", 0, j), "s", block // 2)],
        )
        for e in (1, 3):
            sends = [(("s", e, j), "s", block // 2)]
            if (e == 1) == (j in (0, 3)):
                sends.append((("x", 2, j), ("x", e // 2), block))
            plan.add(("xfwd", e, j), (0, 5), needs=[("x", e, j)], sends=sends)
        plan.add(("xfwd", 2, j), (0, 5), needs=[("x", 2, j)], sends=[(("s", 2, j), "s", block // 2)])
    for e in range(X):
        for k in range(CORES):
            needs = [("s", e, j) if k else ("x", e, j) for j in range(Y)]
            if (e, k) == (0, 0):
                needs = [("a", j) for j in range(1, Y)]
            plan.add(("aconv", e, k), (3,), after=[("acopy",)], needs=needs, cost=0.5)
    for w, wave in enumerate(WAVES):
        width = len(wave) * BLOCK
        for d in range(Z):
            needs = [arrival_of(q, d) for q in wave] if d else []
            after = [("mask", q) for q in wave]
            after += [("mm", w - 2, j) for j in range(Y)] if w >= 2 else []
            plan.add(("pconv", w, d), (4, w), after=after, needs=needs, cost=0.15)
        half = ROWS // 2 * width * 4 * CORES
        after = [("pconv", w, d) for d in range(Z)] + [("aconv", e, k) for e in range(X) for k in range(CORES)]
        for j, sends in (
            (2, [(("r1", w, 0), ("y", 0), half), (("r1", w, 1), ("y", 1), half)]),
            (1, [(("r2", w, 0, 1), ("y", 0), half)]),
            (3, [(("r2", w, 1, 0), ("y", 1), half)]),
            (0, []),
        ):
            plan.add(("mm", w, j), (5, w, (2, 1, 3, 0).index(j)), after=after, sends=sends, cost=1.1)
        for way in range(2):
            plan.add(
                ("radd", w, way), (2, 0), after=[("mm", w, 1 + 2 * way)], needs=[("r1", w, way)],
                sends=[(("r2", w, way, way), ("y", way), half)], cost=0.1,
            )
        plan.add(
            ("fin", w), (2, 1), after=[("mm", w, 0), ("radd", w, 0), ("radd", w, 1)],
            needs=[("r2", w, way, h) for way in range(2) for h in range(2)], cost=0.8,
        )
    for g in range(GROUPS):
        owners = [("fin", w) for w, wave in enumerate(WAVES) if set(wave) & {2 * g, 2 * g + 1}]
        plan.add(("d1", g), (2, 2), after=owners, sends=[(("d1", g, j), None, 0) for j in (1, 3, 2)])
        plan.add(
            ("d2", g), (2, 2), needs=[("d1", g, j) for j in range(1, Y)],
            sends=[(("d2", g, i), None, 0) for i in range(1, Z)], cost=0.1,
        )
        plan.add(
            ("d3", g), (2, 2), needs=[("d2", g, i) for i in range(1, Z)],
            sends=[(("d3", g, i), None, 0) for i in range(1, Z)], cost=0.1,
        )
        plan.add(
            ("d4", g), (2, 2), needs=[("d3", g, i) for i in range(1, Z)],
            sends=[(("d4", g, j), None, 0) for j in range(1, Y)],
        )
        plan.add(("d5", g), (2, 2), needs=[("d4", g, j) for j in range(1, Y)], cost=0.1)
    return plan


def split(v):
    high = v.astype(jnp.bfloat16)
    return high, (v - high.astype(jnp.float32)).astype(jnp.bfloat16)


def dot(a, b):
    return jnp.dot(a, b, preferred_element_type=jnp.float32)


def kernel(order, a_ref, p_ref, fill_ref, d_ref, x_ref, g_ref, *scratch):
    (agat, ahi, alo, pgat, phi, plo, t, dr1, s1, dr2, res, send_sem, recv_sem), waves = scratch[:13], scratch[13:]
    xp, xr1, xr2 = waves[0::3], waves[1::3], waves[2::3]
    r, c = lax.axis_index("row"), lax.axis_index("col")
    z, y, x, core = lax.div(r, Y), lax.rem(r, Y), lax.div(c, CORES), lax.rem(c, CORES)

    def device(dz=0, dy=0, dx=0, dc=0):
        return {
            "row": lax.rem(z + dz, Z) * Y + lax.rem(y + dy, Y),
            "col": lax.rem(x + dx, X) * CORES + lax.rem(core + dc, CORES),
        }

    def part(index, size):
        return pl.ds(pl.multiple_of(index * size, size), size)

    partners = [device(dz=i) for i in range(1, Z)] + [device(dy=j) for j in range(1, Y)]
    partners += [device(dx=1), device(dx=X - 1), device(dc=1)]
    barrier = pltpu.get_barrier_semaphore()
    for partner in partners:
        pl.semaphore_signal(barrier, inc=1, device_id=partner, device_id_type=pl.DeviceIdType.MESH)
    pl.semaphore_wait(barrier, len(partners))

    half, quarter, eighth = ROWS // 2, 2 * BLOCK // Y, 2 * BLOCK // Y // Z

    def ends(ident):
        kind, *at = ident
        if kind == "z":
            way, q, s = at
            return (
                pgat.at[q, zslot(way, s)], pgat.at[q, zslot(way, s + 1)],
                device(dz=1 if way == 0 else Z - 1),
            )
        if kind == "a":
            (j,) = at
            i = Y - j
            return a_ref.at[:, part(lax.rem(y + i, Y), ROWS)], agat.at[0, 0, j], device(dy=i)
        if kind == "x":
            e, j = at
            if e == 2:
                way = 0 if j in (0, 3) else 1
                source = agat.at[1 + 2 * way, 0, j]
            else:
                way, source = e // 2, agat.at[0, 0, j]
            return source, agat.at[e, 0, j], device(dx=1 if way == 0 else X - 1)
        if kind == "s":
            e, j = at
            return agat.at[e, 0, j], agat.at[e, 1, j], device(dc=1)
        if kind == "r1":
            w, way = at
            return xp[w].at[2, pl.ds(way * half, half)], xr1[w].at[way], device(dy=1 if way == 0 else Y - 1)
        if kind == "r2":
            w, way, h = at
            rows = pl.ds(h * half, half)
            return xp[w].at[1 + 2 * way, rows], xr2[w].at[way, rows], device(dy=1 if way == 0 else Y - 1)
        if kind == "d1":
            g, j = at
            return t.at[g, part(lax.rem(y + j, Y), quarter)], dr1.at[g, j - 1], device(dy=j)
        if kind == "d2":
            g, i = at
            return s1.at[g, part(lax.rem(z + i, Z), eighth)], dr2.at[g, i - 1], device(dz=i)
        if kind == "d3":
            g, i = at
            where = res.at[g, y, part(z, eighth)]
            return where, where, device(dz=i)
        g, j = at
        return res.at[g, y], res.at[g, y], device(dy=j)

    def fill(q, i):
        return fill_ref[q, 2 * r + i].astype(jnp.float32)

    def body(name):
        kind, *at = name
        if kind == "mask":
            (q,) = at
            for i in range(2):
                rows = slice(i * BLOCK, (i + 1) * BLOCK)
                pgat[q, 0, rows] = p_ref[rows, q * BLOCK : (q + 1) * BLOCK] * fill(q, i)
        elif kind == "acopy":
            agat[0, 0, 0] = a_ref[:, part(y, ROWS)]
        elif kind == "aconv":
            e, k = at
            owner = lax.rem(x + X - e, X) * CORES + lax.rem(core + k, CORES)
            place = part(lax.rem(z + Z - owner, Z), ROWS)

            @pl.loop(0, Y)
            def _(j):
                high, low = split(agat[e, k, j])
                ahi[part(j, ROWS), place] = high
                alo[part(j, ROWS), place] = low

        elif kind == "pconv":
            w, d = at
            for i, q in enumerate(WAVES[w]):
                high, low = split(pgat[q, d])
                phi[w % 2, d * ROWS : (d + 1) * ROWS, i * BLOCK : (i + 1) * BLOCK] = high
                plo[w % 2, d * ROWS : (d + 1) * ROWS, i * BLOCK : (i + 1) * BLOCK] = low
        elif kind == "mm":
            w, j = at
            cols = slice(0, len(WAVES[w]) * BLOCK)
            rows = slice(j * ROWS, (j + 1) * ROWS)
            high, low = phi[w % 2, :, cols], plo[w % 2, :, cols]
            xp[w][j] = dot(ahi[rows], high) + dot(ahi[rows], low) + dot(alo[rows], high)
        elif kind == "radd":
            w, way = at
            rows = slice(way * half, (way + 1) * half)
            xp[w][1 + 2 * way, rows] += xr1[w][way]
        elif kind == "fin":
            (w,) = at
            total = xp[w][0] + xr2[w][0] + xr2[w][1]
            for n, q in enumerate(WAVES[w]):
                mine = total[:, n * BLOCK : (n + 1) * BLOCK]
                mine = jnp.concatenate([mine[i * BLOCK : (i + 1) * BLOCK] * -fill(q, i) for i in range(2)], axis=0)
                x_ref[:, q * BLOCK : (q + 1) * BLOCK] = mine
                t[q // 2, q % 2 * BLOCK : (q % 2 + 1) * BLOCK] = lax.dot_general(
                    pgat[q, 0], mine, (((0,), (0,)), ((), ())),
                    precision=lax.Precision.HIGHEST, preferred_element_type=jnp.float32,
                )
        elif kind == "d2":
            (g,) = at
            s1[g] = t[g, part(y, quarter)] + dr1[g, 0] + dr1[g, 1] + dr1[g, 2]
        elif kind == "d3":
            (g,) = at
            total = s1[g, part(z, eighth)]
            for i in range(Z - 1):
                total += dr2[g, i]
            res[g, y, part(z, eighth)] = total
        elif kind == "d5":
            (g,) = at
            rows = slice(2 * g * BLOCK, 2 * (g + 1) * BLOCK)
            g_ref[rows] = d_ref[rows] - res[g].reshape(2 * BLOCK, BLOCK)

    copies = {}
    waited = set()
    for _, task in order:
        for ident in task["needs"]:
            if ident not in waited:
                waited.add(ident)
                copies[ident].wait_recv()
        body(task["name"])
        for ident, _, _ in task["sends"]:
            source, target, where = ends(ident)
            n = len(copies)
            copies[ident] = pltpu.make_async_remote_copy(
                src_ref=source, dst_ref=target, send_sem=send_sem.at[n], recv_sem=recv_sem.at[n],
                device_id=where, device_id_type=pl.DeviceIdType.MESH,
            )
            copies[ident].start()
    for ident, copy in copies.items():
        if ident not in waited:
            copy.wait_recv()
        copy.wait_send()


def local(top_inverse, panels, fill_pattern, diagonal_part):
    order, _ = make_plan().order()
    count = sum(len(task["sends"]) for _, task in order)
    f32, bf16 = jnp.float32, jnp.bfloat16
    depth = Z * ROWS
    scratch = [
        pltpu.VMEM((X, CORES, Y, ROWS, ROWS), f32),
        pltpu.VMEM((Y * ROWS, depth), bf16),
        pltpu.VMEM((Y * ROWS, depth), bf16),
        pltpu.VMEM((CHUNKS, Z, ROWS, BLOCK), f32),
        pltpu.VMEM((2, depth, 2 * BLOCK), bf16),
        pltpu.VMEM((2, depth, 2 * BLOCK), bf16),
        pltpu.VMEM((GROUPS, 2 * BLOCK, BLOCK), f32),
        pltpu.VMEM((GROUPS, Y - 1, 2 * BLOCK // Y, BLOCK), f32),
        pltpu.VMEM((GROUPS, 2 * BLOCK // Y, BLOCK), f32),
        pltpu.VMEM((GROUPS, Z - 1, 2 * BLOCK // Y // Z, BLOCK), f32),
        pltpu.VMEM((GROUPS, Y, 2 * BLOCK // Y, BLOCK), f32),
        pltpu.SemaphoreType.DMA((count,)),
        pltpu.SemaphoreType.DMA((count,)),
    ]
    for wave in WAVES:
        width = len(wave) * BLOCK
        scratch += [
            pltpu.VMEM((Y, ROWS, width), f32),
            pltpu.VMEM((2, ROWS // 2, width), f32),
            pltpu.VMEM((2, ROWS, width), f32),
        ]
    vmem = pl.BlockSpec(memory_space=pltpu.VMEM)
    return pl.pallas_call(
        functools.partial(kernel, order),
        out_shape=(jax.ShapeDtypeStruct(panels.shape, f32), jax.ShapeDtypeStruct(diagonal_part.shape, f32)),
        in_specs=[vmem, vmem, pl.BlockSpec(memory_space=pltpu.SMEM), vmem],
        out_specs=(vmem, vmem),
        scratch_shapes=scratch,
        compiler_params=pltpu.CompilerParams(
            collective_id=0, has_side_effects=True, vmem_limit_bytes=60 * 1024 * 1024
        ),
        cost_estimate=pl.CostEstimate(flops=2 * 8192**3 // 256, bytes_accessed=5 * 2**20, transcendentals=0),
        name="selected_inverse",
    )(top_inverse, panels, fill_pattern, diagonal_part)


def solution(mesh):
    in_specs = (P("row", "col"), P("row", "col"), P("col", None), P("col", None))
    out_specs = (P("row", "col"), P("col", None))
    return jax.shard_map(local, mesh=mesh, in_specs=in_specs, out_specs=out_specs, check_vma=False)
```

```python
import functools

import jax
import jax.numpy as jnp
from jax import lax
from jax.experimental import pallas as pl
from jax.experimental.pallas import tpu as pltpu
from jax.sharding import PartitionSpec as P

BLOCK = 128
Z, Y, X, CORES = 8, 4, 4, 2
ROWS = 2 * BLOCK
CHUNKS = 8
WAVES = ((0, 1), (2, 3), (4,), (5,), (6,), (7,))
GROUPS = 4
EARLY = (4, 5, 6, 7)
TURNS = ((0, 1, 2, 3, 4, 6, 7, 5), (0, 1, 3, 4, 2, 5, 6, 7))
GATE = 1.500
LONG = (0, 1, 0, 1, 1, 1, 0, 0)
LINK = 96e3
HOP = 3.0


def steps(way, q):
    return 4 if LONG[q] == way else 3


def zslot(way, s):
    return s if way == 0 else (Z - s) % Z


def arrival_of(q, d):
    if d < 4 or (d == 4 and LONG[q] == 0):
        return ("z", 0, q, d - 1)
    return ("z", 1, q, Z - 1 - d)


def near_slots(q):
    return (5, 6, 7) if LONG[q] else (1, 2, 3)


def far_slots(q):
    return (1, 2, 3) if LONG[q] else (5, 6, 7)


class Plan:
    def __init__(self):
        self.tasks = []

    def add(self, name, rank, after=(), needs=(), sends=(), cost=0.0, gate=None):
        self.tasks.append(
            dict(name=name, rank=rank, after=after, needs=needs, sends=sends, cost=cost, gate=gate)
        )

    def order(self):
        now, free, arrived, done, result = 0.0, {}, {}, set(), []
        left = list(self.tasks)
        while left:
            best = None
            for task in left:
                if not all(n in done for n in task["after"]) or not all(n in arrived for n in task["needs"]):
                    continue
                ready = max([arrived[n] for n in task["needs"]], default=0.0)
                if task["gate"] is not None:
                    link, depth = task["gate"]
                    ready = max(ready, free.get(link, 0.0) - depth)
                ready = max(ready, now)
                key = (ready, task["rank"])
                if best is None or key < best[0]:
                    best = (key, task)
            (ready, _), task = best
            now = ready + task["cost"]
            for ident, link, size in task["sends"]:
                now += 0.09
                if link[0] == "far":
                    free[link[1]] = max(now, free.get(link[1], 0.0)) + size / LINK
                    arrived[ident] = max(now, free[link[1]]) + (4.0 if link[1][0] == "z" else 3.5)
                else:
                    rate = 6 * LINK if link == "s" else LINK
                    begin = max(now, free.get(link, 0.0))
                    free[link] = begin + size / rate
                    arrived[ident] = free[link] + HOP
                    task.setdefault("sent", []).append((ident, free[link]))
            done.add(task["name"])
            left.remove(task)
            result.append((ready, task))
        return result, now


def make_plan():
    plan = Plan()
    piece = ROWS * BLOCK * 4 * CORES
    for q in range(CHUNKS):
        plan.add(("mask", q), (1, q) if q else (0, 0), cost=0.15)
        for way in range(2):
            turn = TURNS[way].index(q)
            plan.add(
                ("zown", way, q), (0, 1, way) if q == 0 else (2, turn, way),
                after=[("mask", q)] + ([("zown", way, TURNS[way][turn - 1])] if turn else []),
                sends=[(("z", way, q, 0), ("z", way), piece)], gate=(("z", way), GATE),
            )
            for s in range(1, steps(way, q)):
                plan.add(
                    ("zfwd", way, q, s), (1, turn, s), needs=[("z", way, q, s - 1)],
                    sends=[(("z", way, q, s), ("z", way), piece)],
                )
    block = ROWS * ROWS * 4 * CORES
    plan.add(
        ("a2a",), (0, 2),
        sends=[(("a", 3), ("y", 0), block), (("a", 1), ("y", 1), block), (("a", 2), ("y", 0), 2 * block)],
    )
    plan.add(("acopy",), (0, 3), cost=0.15)
    for j in range(Y):
        plan.add(
            ("xown", j), (0, 4), after=[("acopy",)], needs=[("a", j)] if j else [],
            sends=[(("x", 1, j), ("x", 0), block), (("x", 3, j), ("x", 1), block), (("s", 0, j), "s", block // 2)],
        )
        for e in (1, 3):
            sends = [(("s", e, j), "s", block // 2)]
            if (e == 1) == (j in (0, 3)):
                sends.append((("x", 2, j), ("x", e // 2), block))
            plan.add(("xfwd", e, j), (0, 5), needs=[("x", e, j)], sends=sends)
        plan.add(("xfwd", 2, j), (0, 5), needs=[("x", 2, j)], sends=[(("s", 2, j), "s", block // 2)])
    for e in range(X):
        for k in range(CORES):
            needs = [("s", e, j) if k else ("x", e, j) for j in range(Y)]
            if (e, k) == (0, 0):
                needs = [("a", j) for j in range(1, Y)]
            plan.add(("aconv", e, k), (3,), after=[("acopy",)], needs=needs, cost=0.5)
    for q in EARLY:
        plan.add(
            ("share", q), (6, q), after=[("mask", q)], gate=(("y", q % 2), 0.0),
            sends=[(("p", q, 3), ("y", 0), piece), (("p", q, 1), ("y", 1), piece)],
        )
        plan.add(
            ("relay", q), (6, q), needs=[("p", q, 1 if q % 2 else 3)],
            sends=[(("p", q, 2), ("y", q % 2), piece)],
        )
    for w, wave in enumerate(WAVES):
        width = len(wave) * BLOCK
        for d in range(Z):
            needs = [arrival_of(q, d) for q in wave] if d else []
            after = [("mask", q) for q in wave]
            plan.add(("pconv", w, d), (4, w), after=after, needs=needs, cost=0.15)
        half = ROWS // 2 * width * 4 * CORES
        after = [("aconv", e, k) for e in range(X) for k in range(CORES)]
        early = wave[0] in EARLY
        for j in range(Y):
            before = after + [("pconv", w, d) for d in (0,) + near_slots(wave[0])]
            before += [("early", w - 2)] if w >= 2 and WAVES[w - 2][0] in EARLY else []
            plan.add(("near", w, j), (5, w, j), after=before if early else [], cost=(0.2 + 0.15 * len(wave)) if early else 0.0)
            before = [("near", w, j), ("pconv", w, 4)]
            plan.add(("join", w, j), (2, w, j), after=before if early else [], cost=(0.1 + 0.05 * len(wave)) if early else 0.0)
        if early:
            plan.add(
                ("early", w), (2, 2), after=[("join", w, j) for j in range(Y)],
                needs=[("p", q, j) for q in wave for j in range(1, Y)], cost=0.7 * len(wave),
            )
        after += [("pconv", w, d) for d in range(Z)] + [("join", w, j) for j in range(Y)]
        for j, sends in (
            (2, [(("r1", w, 0), ("y", 0), half), (("r1", w, 1), ("y", 1), half)]),
            (1, [(("r2", w, 0, 1), ("y", 0), half)]),
            (3, [(("r2", w, 1, 0), ("y", 1), half)]),
            (0, []),
        ):
            plan.add(("mm", w, j), (5, w, (2, 1, 3, 0).index(j)), after=after, sends=sends, cost=(0.2 + 0.1 * len(wave)) if early else 0.75)
        for way in range(2):
            plan.add(
                ("radd", w, way), (2, 0), after=[("mm", w, 1 + 2 * way)], needs=[("r1", w, way)],
                sends=[(("r2", w, way, way), ("y", way), half)], cost=0.1,
            )
        plan.add(
            ("fin", w), (2, 1), after=[("mm", w, 0), ("radd", w, 0), ("radd", w, 1)],
            needs=[("r2", w, way, h) for way in range(2) for h in range(2)], cost=0.8,
        )
    small = 2 * BLOCK // Y * BLOCK * 4 * CORES
    for g in range(GROUPS):
        stage = "early" if 2 * g in EARLY else "fin"
        owners = [(stage, w) for w, wave in enumerate(WAVES) if set(wave) & {2 * g, 2 * g + 1}]
        plan.add(("d1", g), (2, 2), after=owners, sends=[(("d1", g, j), ("far", ("y", j // 2)), small * min(j, Y - j)) for j in (2, 1, 3)])
        plan.add(
            ("d2", g), (2, 2), needs=[("d1", g, j) for j in range(1, Y)],
            sends=[(("d2", g, i), ("far", ("z", i // 4)), small // Z * min(i, Z - i)) for i in (4, 3, 5, 2, 6, 1, 7)], cost=0.1,
        )
        plan.add(
            ("d3", g), (2, 2), needs=[("d2", g, i) for i in range(1, Z)],
            sends=[(("d3", g, i), ("far", ("z", i // 4)), small // Z * min(i, Z - i)) for i in (4, 3, 5, 2, 6, 1, 7)], cost=0.1,
        )
        plan.add(
            ("d4", g), (2, 2), needs=[("d3", g, i) for i in range(1, Z)],
            sends=[(("d4", g, j), ("far", ("y", j // 2)), small * min(j, Y - j)) for j in range(1, Y)],
        )
        plan.add(("d5", g), (2, 2), needs=[("d4", g, j) for j in range(1, Y)], cost=0.1)
    return plan


def split(v):
    high = v.astype(jnp.bfloat16)
    return high, (v - high.astype(jnp.float32)).astype(jnp.bfloat16)


def outer(a, b):
    return lax.dot_general(
        a, b, (((0,), (0,)), ((), ())), precision=lax.Precision.HIGHEST, preferred_element_type=jnp.float32
    )


def dot(a, b):
    return jnp.dot(a, b, preferred_element_type=jnp.float32)


def kernel(order, a_any, p_any, fill_ref, x_any, g_any, a_ref, p_ref, x_ref, *scratch):
    (agat, ahi, alo, pgat, phi, plo, py, yh, t, dr1, s1, dr2, res, send_sem, recv_sem, in_sem, out_sem) = scratch[:17]
    waves = scratch[17:]
    xp, xr1, xs, xr2 = waves[0::4], waves[1::4], waves[2::4], waves[3::4]
    r, c = lax.axis_index("row"), lax.axis_index("col")
    z, y, x, core = lax.div(r, Y), lax.rem(r, Y), lax.div(c, CORES), lax.rem(c, CORES)

    def device(dz=0, dy=0, dx=0, dc=0):
        return {
            "row": lax.rem(z + dz, Z) * Y + lax.rem(y + dy, Y),
            "col": lax.rem(x + dx, X) * CORES + lax.rem(core + dc, CORES),
        }

    def part(index, size):
        return pl.ds(pl.multiple_of(index * size, size), size)

    partners = [device(dz=i) for i in range(1, Z)] + [device(dy=j) for j in range(1, Y)]
    partners += [device(dx=1), device(dx=X - 1), device(dc=1)]
    barrier = pltpu.get_barrier_semaphore()
    for partner in partners:
        pl.semaphore_signal(barrier, inc=1, device_id=partner, device_id_type=pl.DeviceIdType.MESH)
    inputs = [pltpu.make_async_copy(p_any, p_ref, in_sem.at[0]), pltpu.make_async_copy(a_any, a_ref, in_sem.at[1])]
    for copy in inputs:
        copy.start()
    outputs = []

    def write(source, target):
        copy = pltpu.make_async_copy(source, target, out_sem.at[len(outputs)])
        copy.start()
        outputs.append(copy)

    half, quarter, eighth = ROWS // 2, 2 * BLOCK // Y, 2 * BLOCK // Y // Z

    def ends(ident):
        kind, *at = ident
        if kind == "z":
            way, q, s = at
            return (
                pgat.at[q, zslot(way, s)], pgat.at[q, zslot(way, s + 1)],
                device(dz=1 if way == 0 else Z - 1),
            )
        if kind == "a":
            (j,) = at
            i = Y - j
            return a_ref.at[:, part(lax.rem(y + i, Y), ROWS)], agat.at[0, 0, j], device(dy=i)
        if kind == "x":
            e, j = at
            if e == 2:
                way = 0 if j in (0, 3) else 1
                source = agat.at[1 + 2 * way, 0, j]
            else:
                way, source = e // 2, agat.at[0, 0, j]
            return source, agat.at[e, 0, j], device(dx=1 if way == 0 else X - 1)
        if kind == "s":
            e, j = at
            return agat.at[e, 0, j], agat.at[e, 1, j], device(dc=1)
        if kind == "p":
            q, j = at
            source, where = pgat.at[q, 0], device(dy=Y - j)
            if j == 2:
                source = py.at[q - EARLY[0], 0 if q % 2 else 2]
                where = device(dy=Y - 1 if q % 2 else 1)
            return source, py.at[q - EARLY[0], j - 1], where
        if kind == "r1":
            w, way = at
            return xp[w].at[2, pl.ds(way * half, half)], xr1[w].at[way], device(dy=1 if way == 0 else Y - 1)
        if kind == "r2":
            w, way, h = at
            rows = pl.ds(h * half, half)
            source = xs[w].at[way] if h == way else xp[w].at[1 + 2 * way, rows]
            return source, xr2[w].at[way, rows], device(dy=1 if way == 0 else Y - 1)
        if kind == "d1":
            g, j = at
            return t.at[g, part(lax.rem(y + j, Y), quarter)], dr1.at[g, j - 1], device(dy=j)
        if kind == "d2":
            g, i = at
            return s1.at[g, part(lax.rem(z + i, Z), eighth)], dr2.at[g, i - 1], device(dz=i)
        if kind == "d3":
            g, i = at
            where = res.at[g, y, part(z, eighth)]
            return where, where, device(dz=i)
        g, j = at
        return res.at[g, y], res.at[g, y], device(dy=j)

    def fill(q, i):
        return fill_ref[q, 2 * r + i].astype(jnp.float32)

    def product(w, j, slot, count):
        cols = slice(0, len(WAVES[w]) * BLOCK)
        rows, depth = slice(j * ROWS, (j + 1) * ROWS), slice(slot * ROWS, (slot + count) * ROWS)
        high, low = phi[w, depth, cols], plo[w, depth, cols]
        return dot(ahi[rows, depth], high) + dot(ahi[rows, depth], low) + dot(alo[rows, depth], high)

    def body(name):
        kind, *at = name
        if kind == "mask":
            (q,) = at
            for i in range(2):
                rows = slice(i * BLOCK, (i + 1) * BLOCK)
                pgat[q, 0, rows] = p_ref[rows, q * BLOCK : (q + 1) * BLOCK] * fill(q, i)
        elif kind == "acopy":
            agat[0, 0, 0] = a_ref[:, part(y, ROWS)]
        elif kind == "aconv":
            e, k = at
            owner = lax.rem(x + X - e, X) * CORES + lax.rem(core + k, CORES)
            place = part(lax.rem(z + Z - owner, Z), ROWS)

            @pl.loop(0, Y)
            def _(j):
                high, low = split(agat[e, k, j])
                ahi[part(j, ROWS), place] = high
                alo[part(j, ROWS), place] = low

        elif kind == "pconv":
            w, d = at
            for i, q in enumerate(WAVES[w]):
                high, low = split(pgat[q, d])
                phi[w, d * ROWS : (d + 1) * ROWS, i * BLOCK : (i + 1) * BLOCK] = high
                plo[w, d * ROWS : (d + 1) * ROWS, i * BLOCK : (i + 1) * BLOCK] = low
        elif kind == "mm":
            w, j = at
            if WAVES[w][0] in EARLY:
                xp[w][j] += product(w, j, far_slots(WAVES[w][0])[0], 3)
            else:
                xp[w][j] = product(w, j, 0, Z)
        elif kind == "near":
            w, j = at
            if WAVES[w][0] in EARLY:
                own = product(w, j, 0, 1)
                near = product(w, j, near_slots(WAVES[w][0])[0], 3)
                xp[w][j] = own + near
                yh[w % 2, j, :, : len(WAVES[w]) * BLOCK] = 0.5 * own + near
        elif kind == "join":
            w, j = at
            if WAVES[w][0] in EARLY:
                opposite = product(w, j, 4, 1)
                xp[w][j] += opposite
                yh[w % 2, j, :, : len(WAVES[w]) * BLOCK] += 0.5 * opposite
        elif kind == "radd":
            w, way = at
            rows = slice(way * half, (way + 1) * half)
            xs[w][way] = xp[w][1 + 2 * way, rows] + xr1[w][way]
        elif kind == "early":
            (w,) = at
            for n, q in enumerate(WAVES[w]):
                cols = slice(n * BLOCK, (n + 1) * BLOCK)
                total = outer(pgat[q, 0], yh[w % 2, 0, :, cols])
                for j in range(1, Y):
                    total += outer(py[q - EARLY[0], j - 1], yh[w % 2, j, :, cols])
                t[q // 2, q % 2 * BLOCK : (q % 2 + 1) * BLOCK] = total + total.T
        elif kind == "fin":
            (w,) = at
            total = xp[w][0] + xr2[w][0] + xr2[w][1]
            for n, q in enumerate(WAVES[w]):
                mine = total[:, n * BLOCK : (n + 1) * BLOCK]
                mine = jnp.concatenate([mine[i * BLOCK : (i + 1) * BLOCK] * fill(q, i) for i in range(2)], axis=0)
                x_ref[:, q * BLOCK : (q + 1) * BLOCK] = mine
                if q not in EARLY:
                    t[q // 2, q % 2 * BLOCK : (q % 2 + 1) * BLOCK] = outer(pgat[q, 0], mine)
            cols = slice(WAVES[w][0] * BLOCK, (WAVES[w][-1] + 1) * BLOCK)
            write(x_ref.at[:, cols], x_any.at[:, cols])
        elif kind == "d2":
            (g,) = at
            s1[g] = t[g, part(y, quarter)] + dr1[g, 0] + dr1[g, 1] + dr1[g, 2]
        elif kind == "d3":
            (g,) = at
            total = s1[g, part(z, eighth)]
            for i in range(Z - 1):
                total += dr2[g, i]
            res[g, y, part(z, eighth)] = total
        elif kind == "d5":
            (g,) = at
            write(res.at[g], g_any.at[g])

    copies = {}
    waited = set()
    sent = []
    for now, task in order:
        while sent and sent[0][0] < now - 3.0:
            copies[sent.pop(0)[1]].wait_send()
        if task["name"] == ("mask", 0):
            inputs[0].wait()
        if task["name"] == ("a2a",):
            inputs[1].wait()
        for ident in task["needs"]:
            if ident not in waited:
                waited.add(ident)
                copies[ident].wait_recv()
        body(task["name"])
        for ident, _, _ in task["sends"]:
            source, target, where = ends(ident)
            n = len(copies)
            if n == 0:
                pl.semaphore_wait(barrier, len(partners))
            copies[ident] = pltpu.make_async_remote_copy(
                src_ref=source, dst_ref=target, send_sem=send_sem.at[n], recv_sem=recv_sem.at[n],
                device_id=where, device_id_type=pl.DeviceIdType.MESH,
            )
            copies[ident].start()
            sent.append((now if ident[0][0] == "d" else dict(task["sent"])[ident], ident))
        sent.sort(key=lambda entry: entry[0])
    for _, ident in sent:
        copies[ident].wait_send()
    for ident, copy in copies.items():
        if ident not in waited:
            copy.wait_recv()
    for copy in outputs:
        copy.wait()


def local(top_inverse, panels, fill_pattern, diagonal_part):
    order, _ = make_plan().order()
    count = sum(len(task["sends"]) for _, task in order)
    f32, bf16 = jnp.float32, jnp.bfloat16
    depth = Z * ROWS
    scratch = [
        pltpu.VMEM((ROWS, Y * ROWS), f32),
        pltpu.VMEM((ROWS, CHUNKS * BLOCK), f32),
        pltpu.VMEM((ROWS, CHUNKS * BLOCK), f32),
        pltpu.VMEM((X, CORES, Y, ROWS, ROWS), f32),
        pltpu.VMEM((Y * ROWS, depth), bf16),
        pltpu.VMEM((Y * ROWS, depth), bf16),
        pltpu.VMEM((CHUNKS, Z, ROWS, BLOCK), f32),
        pltpu.VMEM((len(WAVES), depth, 2 * BLOCK), bf16),
        pltpu.VMEM((len(WAVES), depth, 2 * BLOCK), bf16),
        pltpu.VMEM((len(EARLY), Y - 1, ROWS, BLOCK), f32),
        pltpu.VMEM((2, Y, ROWS, 2 * BLOCK), f32),
        pltpu.VMEM((GROUPS, 2 * BLOCK, BLOCK), f32),
        pltpu.VMEM((GROUPS, Y - 1, 2 * BLOCK // Y, BLOCK), f32),
        pltpu.VMEM((GROUPS, 2 * BLOCK // Y, BLOCK), f32),
        pltpu.VMEM((GROUPS, Z - 1, 2 * BLOCK // Y // Z, BLOCK), f32),
        pltpu.VMEM((GROUPS, Y, 2 * BLOCK // Y, BLOCK), f32),
        pltpu.SemaphoreType.DMA((count,)),
        pltpu.SemaphoreType.DMA((count,)),
        pltpu.SemaphoreType.DMA((2,)),
        pltpu.SemaphoreType.DMA((len(WAVES) + GROUPS,)),
    ]
    for wave in WAVES:
        width = len(wave) * BLOCK
        scratch += [
            pltpu.VMEM((Y, ROWS, width), f32),
            pltpu.VMEM((2, ROWS // 2, width), f32),
            pltpu.VMEM((2, ROWS // 2, width), f32),
            pltpu.VMEM((2, ROWS, width), f32),
        ]
    anywhere = pl.BlockSpec(memory_space=pl.ANY)
    product, terms = pl.pallas_call(
        functools.partial(kernel, order),
        out_shape=(
            jax.ShapeDtypeStruct(panels.shape, f32),
            jax.ShapeDtypeStruct((GROUPS, Y, 2 * BLOCK // Y, BLOCK), f32),
        ),
        in_specs=[anywhere, anywhere, pl.BlockSpec(memory_space=pltpu.SMEM)],
        out_specs=(anywhere, anywhere),
        scratch_shapes=scratch,
        compiler_params=pltpu.CompilerParams(
            collective_id=0, has_side_effects=True, vmem_limit_bytes=60 * 1024 * 1024
        ),
        cost_estimate=pl.CostEstimate(flops=2 * 8192**3 // 256, bytes_accessed=5 * 2**20, transcendentals=0),
        name="selected_inverse",
    )(top_inverse, panels, fill_pattern)
    return -product, diagonal_part + terms.reshape(diagonal_part.shape)


def solution(mesh):
    in_specs = (P("row", "col"), P("row", "col"), P("col", None), P("col", None))
    out_specs = (P("row", "col"), P("col", None))
    return jax.shard_map(local, mesh=mesh, in_specs=in_specs, out_specs=out_specs, check_vma=False)
```

```python
import functools

import jax
import jax.numpy as jnp
from jax import lax
from jax.experimental import pallas as pl
from jax.experimental.pallas import tpu as pltpu
from jax.sharding import PartitionSpec as P

BLOCK = 128
Z, Y, X, CORES = 8, 4, 4, 2
ROWS = 2 * BLOCK
CHUNKS = 8
WAVES = ((0, 1), (2, 3), (4,), (5,), (6,), (7,))
GROUPS = 4
EARLY = (4, 5, 6, 7)
TURNS = ((0, 1, 2, 3, 4, 6, 7, 5), (0, 1, 3, 4, 2, 5, 6, 7))
GATE = 1.500
LONG = (0, 1, 0, 1, 1, 1, 0, 0)
LINK = 96e3
HOP = 3.0


def steps(way, q):
    return 4 if LONG[q] == way else 3


def zslot(way, s):
    return s if way == 0 else (Z - s) % Z


def arrival_of(q, d):
    if d < 4 or (d == 4 and LONG[q] == 0):
        return ("z", 0, q, d - 1)
    return ("z", 1, q, Z - 1 - d)


def near_slots(q):
    return (5, 6, 7) if LONG[q] else (1, 2, 3)


def far_slots(q):
    return (1, 2, 3) if LONG[q] else (5, 6, 7)


class Plan:
    def __init__(self):
        self.tasks = []

    def add(self, name, rank, after=(), needs=(), sends=(), cost=0.0, gate=None):
        self.tasks.append(
            dict(name=name, rank=rank, after=after, needs=needs, sends=sends, cost=cost, gate=gate)
        )

    def order(self):
        now, free, arrived, done, result = 0.0, {}, {}, set(), []
        left = list(self.tasks)
        while left:
            best = None
            for task in left:
                if not all(n in done for n in task["after"]) or not all(n in arrived for n in task["needs"]):
                    continue
                ready = max([arrived[n] for n in task["needs"]], default=0.0)
                if task["gate"] is not None:
                    link, depth = task["gate"]
                    ready = max(ready, free.get(link, 0.0) - depth)
                ready = max(ready, now)
                key = (ready, task["rank"])
                if best is None or key < best[0]:
                    best = (key, task)
            (ready, _), task = best
            now = ready + task["cost"]
            for ident, link, size in task["sends"]:
                now += 0.09
                if link[0] == "far":
                    free[link[1]] = max(now, free.get(link[1], 0.0)) + size / LINK
                    arrived[ident] = max(now, free[link[1]]) + (4.0 if link[1][0] == "z" else 3.5)
                else:
                    rate = 6 * LINK if link == "s" else LINK
                    begin = max(now, free.get(link, 0.0))
                    free[link] = begin + size / rate
                    arrived[ident] = free[link] + HOP
                    task.setdefault("sent", []).append((ident, free[link]))
            done.add(task["name"])
            left.remove(task)
            result.append((ready, task))
        return result, now


def make_plan():
    plan = Plan()
    piece = ROWS * BLOCK * 4 * CORES
    for q in range(CHUNKS):
        plan.add(("mask", q), (1, q) if q else (0, 0), cost=0.15)
        for way in range(2):
            turn = TURNS[way].index(q)
            plan.add(
                ("zown", way, q), (0, 1, way) if q == 0 else (2, turn, way),
                after=[("mask", q)] + ([("zown", way, TURNS[way][turn - 1])] if turn else []),
                sends=[(("z", way, q, 0), ("z", way), piece)], gate=(("z", way), GATE),
            )
            for s in range(1, steps(way, q)):
                plan.add(
                    ("zfwd", way, q, s), (1, turn, s), needs=[("z", way, q, s - 1)],
                    sends=[(("z", way, q, s), ("z", way), piece)],
                )
    block = ROWS * ROWS * 4 * CORES
    plan.add(
        ("a2a",), (0, 2),
        sends=[(("a", 3), ("y", 0), block), (("a", 1), ("y", 1), block), (("a", 2), ("y", 0), 2 * block)],
    )
    plan.add(("acopy",), (0, 3), cost=0.15)
    for j in range(Y):
        plan.add(
            ("xown", j), (0, 4), after=[("acopy",)], needs=[("a", j)] if j else [],
            sends=[(("x", 1, j), ("x", 0), block), (("x", 3, j), ("x", 1), block), (("s", 0, j), "s", block // 2)],
        )
        for e in (1, 3):
            sends = [(("s", e, j), "s", block // 2)]
            if (e == 1) == (j in (0, 3)):
                sends.append((("x", 2, j), ("x", e // 2), block))
            plan.add(("xfwd", e, j), (0, 5), needs=[("x", e, j)], sends=sends)
        plan.add(("xfwd", 2, j), (0, 5), needs=[("x", 2, j)], sends=[(("s", 2, j), "s", block // 2)])
    for e in range(X):
        for k in range(CORES):
            needs = [("s", e, j) if k else ("x", e, j) for j in range(Y)]
            if (e, k) == (0, 0):
                needs = [("a", j) for j in range(1, Y)]
            plan.add(("aconv", e, k), (3,), after=[("acopy",)], needs=needs, cost=0.5)
    for q in EARLY:
        plan.add(
            ("share", q), (6, q), after=[("mask", q)], gate=(("y", q % 2), 0.0),
            sends=[(("p", q, 3), ("y", 0), piece), (("p", q, 1), ("y", 1), piece)],
        )
        plan.add(
            ("relay", q), (6, q), needs=[("p", q, 1 if q % 2 else 3)],
            sends=[(("p", q, 2), ("y", q % 2), piece)],
        )
    for w, wave in enumerate(WAVES):
        width = len(wave) * BLOCK
        for d in range(Z):
            needs = [arrival_of(q, d) for q in wave] if d else []
            after = [("mask", q) for q in wave]
            plan.add(("pconv", w, d), (4, w), after=after, needs=needs, cost=0.15)
        half = ROWS // 2 * width * 4 * CORES
        after = [("aconv", e, k) for e in range(X) for k in range(CORES)]
        early = wave[0] in EARLY
        for j in range(Y):
            before = after + [("pconv", w, d) for d in (0,) + near_slots(wave[0])]
            before += [("early", w - 2)] if w >= 2 and WAVES[w - 2][0] in EARLY else []
            plan.add(("near", w, j), (5, w, j), after=before if early else [], cost=(0.2 + 0.15 * len(wave)) if early else 0.0)
            before = [("near", w, j), ("pconv", w, 4)]
            plan.add(("join", w, j), (2, w, j), after=before if early else [], cost=(0.1 + 0.05 * len(wave)) if early else 0.0)
        if early:
            plan.add(
                ("early", w), (2, 2), after=[("join", w, j) for j in range(Y)],
                needs=[("p", q, j) for q in wave for j in range(1, Y)], cost=0.7 * len(wave),
            )
        after += [("pconv", w, d) for d in range(Z)] + [("join", w, j) for j in range(Y)]
        for j, sends in (
            (2, [(("r1", w, 0), ("y", 0), half), (("r1", w, 1), ("y", 1), half)]),
            (1, [(("r2", w, 0, 1), ("y", 0), half)]),
            (3, [(("r2", w, 1, 0), ("y", 1), half)]),
            (0, []),
        ):
            plan.add(("mm", w, j), (5, w, (2, 1, 3, 0).index(j)), after=after, sends=sends, cost=(0.2 + 0.1 * len(wave)) if early else 0.75)
        for way in range(2):
            plan.add(
                ("radd", w, way), (2, 0), after=[("mm", w, 1 + 2 * way)], needs=[("r1", w, way)],
                sends=[(("r2", w, way, way), ("y", way), half)], cost=0.1,
            )
        plan.add(
            ("fin", w), (2, 1), after=[("mm", w, 0), ("radd", w, 0), ("radd", w, 1)],
            needs=[("r2", w, way, h) for way in range(2) for h in range(2)], cost=0.8,
        )
    small = 2 * BLOCK // Y * BLOCK * 4 * CORES
    for g in range(GROUPS):
        stage = "early" if 2 * g in EARLY else "fin"
        owners = [(stage, w) for w, wave in enumerate(WAVES) if set(wave) & {2 * g, 2 * g + 1}]
        plan.add(("d1", g), (2, 2), after=owners, sends=[(("d1", g, j), ("far", ("y", j // 2)), small * min(j, Y - j)) for j in (2, 1, 3)])
        plan.add(
            ("d2", g), (2, 2), needs=[("d1", g, j) for j in range(1, Y)],
            sends=[(("d2", g, i), ("far", ("z", i // 4)), small // Z * min(i, Z - i)) for i in (4, 3, 5, 2, 6, 1, 7)], cost=0.1,
        )
        plan.add(
            ("d3", g), (2, 2), needs=[("d2", g, i) for i in range(1, Z)],
            sends=[(("d3", g, i), ("far", ("z", i // 4)), small // Z * min(i, Z - i)) for i in (4, 3, 5, 2, 6, 1, 7)], cost=0.1,
        )
        plan.add(
            ("d4", g), (2, 2), needs=[("d3", g, i) for i in range(1, Z)],
            sends=[(("d4", g, j), ("far", ("y", j // 2)), small * min(j, Y - j)) for j in range(1, Y)],
        )
        plan.add(("d5", g), (2, 2), needs=[("d4", g, j) for j in range(1, Y)], cost=0.1)
    return plan


def split(v):
    high = v.astype(jnp.bfloat16)
    return high, (v - high.astype(jnp.float32)).astype(jnp.bfloat16)


def outer(a, b):
    (ah, al), (bh, bl) = split(a), split(b)

    def one(u, v):
        return lax.dot_general(u, v, (((0,), (0,)), ((), ())), preferred_element_type=jnp.float32)

    return one(ah, bh) + one(ah, bl) + one(al, bh)


def dot(a, b):
    return jnp.dot(a, b, preferred_element_type=jnp.float32)


def kernel(order, a_any, p_any, fill_ref, x_any, g_any, a_ref, p_ref, x_ref, *scratch):
    (agat, ahi, alo, pgat, phi, plo, py, yh, t, dr1, s1, dr2, res, send_sem, recv_sem, in_sem, out_sem) = scratch[:17]
    waves = scratch[17:]
    xp, xr1, xs, xr2 = waves[0::4], waves[1::4], waves[2::4], waves[3::4]
    r, c = lax.axis_index("row"), lax.axis_index("col")
    z, y, x, core = lax.div(r, Y), lax.rem(r, Y), lax.div(c, CORES), lax.rem(c, CORES)

    def device(dz=0, dy=0, dx=0, dc=0):
        return {
            "row": lax.rem(z + dz, Z) * Y + lax.rem(y + dy, Y),
            "col": lax.rem(x + dx, X) * CORES + lax.rem(core + dc, CORES),
        }

    def part(index, size):
        return pl.ds(pl.multiple_of(index * size, size), size)

    inputs = [pltpu.make_async_copy(p_any, p_ref, in_sem.at[0]), pltpu.make_async_copy(a_any, a_ref, in_sem.at[1])]
    for copy in inputs:
        copy.start()
    partners = [device(dz=i) for i in range(1, Z)] + [device(dy=j) for j in range(1, Y)]
    partners += [device(dx=1), device(dx=X - 1), device(dc=1)]
    barrier = pltpu.get_barrier_semaphore()
    for partner in partners:
        pl.semaphore_signal(barrier, inc=1, device_id=partner, device_id_type=pl.DeviceIdType.MESH)
    outputs = []

    def write(source, target):
        copy = pltpu.make_async_copy(source, target, out_sem.at[len(outputs)])
        copy.start()
        outputs.append(copy)

    half, quarter, eighth = ROWS // 2, 2 * BLOCK // Y, 2 * BLOCK // Y // Z

    def ends(ident):
        kind, *at = ident
        if kind == "z":
            way, q, s = at
            return (
                pgat.at[q, zslot(way, s)], pgat.at[q, zslot(way, s + 1)],
                device(dz=1 if way == 0 else Z - 1),
            )
        if kind == "a":
            (j,) = at
            i = Y - j
            return a_ref.at[:, part(lax.rem(y + i, Y), ROWS)], agat.at[0, 0, j], device(dy=i)
        if kind == "x":
            e, j = at
            if e == 2:
                way = 0 if j in (0, 3) else 1
                source = agat.at[1 + 2 * way, 0, j]
            else:
                way, source = e // 2, agat.at[0, 0, j]
            return source, agat.at[e, 0, j], device(dx=1 if way == 0 else X - 1)
        if kind == "s":
            e, j = at
            return agat.at[e, 0, j], agat.at[e, 1, j], device(dc=1)
        if kind == "p":
            q, j = at
            source, where = pgat.at[q, 0], device(dy=Y - j)
            if j == 2:
                source = py.at[q - EARLY[0], 0 if q % 2 else 2]
                where = device(dy=Y - 1 if q % 2 else 1)
            return source, py.at[q - EARLY[0], j - 1], where
        if kind == "r1":
            w, way = at
            return xp[w].at[2, pl.ds(way * half, half)], xr1[w].at[way], device(dy=1 if way == 0 else Y - 1)
        if kind == "r2":
            w, way, h = at
            rows = pl.ds(h * half, half)
            source = xs[w].at[way] if h == way else xp[w].at[1 + 2 * way, rows]
            return source, xr2[w].at[way, rows], device(dy=1 if way == 0 else Y - 1)
        if kind == "d1":
            g, j = at
            return t.at[g, part(lax.rem(y + j, Y), quarter)], dr1.at[g, j - 1], device(dy=j)
        if kind == "d2":
            g, i = at
            return s1.at[g, part(lax.rem(z + i, Z), eighth)], dr2.at[g, i - 1], device(dz=i)
        if kind == "d3":
            g, i = at
            where = res.at[g, y, part(z, eighth)]
            return where, where, device(dz=i)
        g, j = at
        return res.at[g, y], res.at[g, y], device(dy=j)

    def fill(q, i):
        return fill_ref[q, 2 * r + i].astype(jnp.float32)

    def product(w, j, slot, count):
        cols = slice(0, len(WAVES[w]) * BLOCK)
        rows, depth = slice(j * ROWS, (j + 1) * ROWS), slice(slot * ROWS, (slot + count) * ROWS)
        high, low = phi[w, depth, cols], plo[w, depth, cols]
        return dot(ahi[rows, depth], high) + dot(ahi[rows, depth], low) + dot(alo[rows, depth], high)

    def body(name):
        kind, *at = name
        if kind == "mask":
            (q,) = at
            for i in range(2):
                rows = slice(i * BLOCK, (i + 1) * BLOCK)
                pgat[q, 0, rows] = p_ref[rows, q * BLOCK : (q + 1) * BLOCK] * fill(q, i)
        elif kind == "acopy":
            agat[0, 0, 0] = a_ref[:, part(y, ROWS)]
        elif kind == "aconv":
            e, k = at
            owner = lax.rem(x + X - e, X) * CORES + lax.rem(core + k, CORES)
            place = part(lax.rem(z + Z - owner, Z), ROWS)

            @pl.loop(0, Y)
            def _(j):
                high, low = split(agat[e, k, j])
                ahi[part(j, ROWS), place] = high
                alo[part(j, ROWS), place] = low

        elif kind == "pconv":
            w, d = at
            for i, q in enumerate(WAVES[w]):
                high, low = split(pgat[q, d])
                phi[w, d * ROWS : (d + 1) * ROWS, i * BLOCK : (i + 1) * BLOCK] = high
                plo[w, d * ROWS : (d + 1) * ROWS, i * BLOCK : (i + 1) * BLOCK] = low
        elif kind == "mm":
            w, j = at
            if WAVES[w][0] in EARLY:
                xp[w][j] += product(w, j, far_slots(WAVES[w][0])[0], 3)
            else:
                xp[w][j] = product(w, j, 0, Z)
        elif kind == "near":
            w, j = at
            if WAVES[w][0] in EARLY:
                own = product(w, j, 0, 1)
                near = product(w, j, near_slots(WAVES[w][0])[0], 3)
                xp[w][j] = own + near
                yh[w % 2, j, :, : len(WAVES[w]) * BLOCK] = 0.5 * own + near
        elif kind == "join":
            w, j = at
            if WAVES[w][0] in EARLY:
                opposite = product(w, j, 4, 1)
                xp[w][j] += opposite
                yh[w % 2, j, :, : len(WAVES[w]) * BLOCK] += 0.5 * opposite
        elif kind == "radd":
            w, way = at
            rows = slice(way * half, (way + 1) * half)
            xs[w][way] = xp[w][1 + 2 * way, rows] + xr1[w][way]
        elif kind == "early":
            (w,) = at
            for n, q in enumerate(WAVES[w]):
                cols = slice(n * BLOCK, (n + 1) * BLOCK)
                total = outer(pgat[q, 0], yh[w % 2, 0, :, cols])
                for j in range(1, Y):
                    total += outer(py[q - EARLY[0], j - 1], yh[w % 2, j, :, cols])
                t[q // 2, q % 2 * BLOCK : (q % 2 + 1) * BLOCK] = total + total.T
        elif kind == "fin":
            (w,) = at
            total = xp[w][0] + xr2[w][0] + xr2[w][1]
            for n, q in enumerate(WAVES[w]):
                mine = total[:, n * BLOCK : (n + 1) * BLOCK]
                mine = jnp.concatenate([mine[i * BLOCK : (i + 1) * BLOCK] * fill(q, i) for i in range(2)], axis=0)
                x_ref[:, q * BLOCK : (q + 1) * BLOCK] = mine
                if q not in EARLY:
                    t[q // 2, q % 2 * BLOCK : (q % 2 + 1) * BLOCK] = outer(pgat[q, 0], mine)
            cols = slice(WAVES[w][0] * BLOCK, (WAVES[w][-1] + 1) * BLOCK)
            write(x_ref.at[:, cols], x_any.at[:, cols])
        elif kind == "d2":
            (g,) = at
            s1[g] = t[g, part(y, quarter)] + dr1[g, 0] + dr1[g, 1] + dr1[g, 2]
        elif kind == "d3":
            (g,) = at
            total = s1[g, part(z, eighth)]
            for i in range(Z - 1):
                total += dr2[g, i]
            res[g, y, part(z, eighth)] = total
        elif kind == "d5":
            (g,) = at
            write(res.at[g], g_any.at[g])

    copies = {}
    waited = set()
    sent = []
    for now, task in order:
        while sent and sent[0][0] < now - 3.0:
            copies[sent.pop(0)[1]].wait_send()
        if task["name"] == ("mask", 0):
            inputs[0].wait()
        if task["name"] == ("a2a",):
            inputs[1].wait()
        for ident in task["needs"]:
            if ident not in waited:
                waited.add(ident)
                copies[ident].wait_recv()
        body(task["name"])
        for ident, _, _ in task["sends"]:
            source, target, where = ends(ident)
            n = len(copies)
            if n == 0:
                pl.semaphore_wait(barrier, len(partners))
            copies[ident] = pltpu.make_async_remote_copy(
                src_ref=source, dst_ref=target, send_sem=send_sem.at[n], recv_sem=recv_sem.at[n],
                device_id=where, device_id_type=pl.DeviceIdType.MESH,
            )
            copies[ident].start()
            sent.append((now if ident[0][0] == "d" else dict(task["sent"])[ident], ident))
        sent.sort(key=lambda entry: entry[0])
    for _, ident in sent:
        copies[ident].wait_send()
    for ident, copy in copies.items():
        if ident not in waited:
            copy.wait_recv()
    for copy in outputs:
        copy.wait()


def local(top_inverse, panels, fill_pattern, diagonal_part):
    order, _ = make_plan().order()
    count = sum(len(task["sends"]) for _, task in order)
    f32, bf16 = jnp.float32, jnp.bfloat16
    depth = Z * ROWS
    scratch = [
        pltpu.VMEM((ROWS, Y * ROWS), f32),
        pltpu.VMEM((ROWS, CHUNKS * BLOCK), f32),
        pltpu.VMEM((ROWS, CHUNKS * BLOCK), f32),
        pltpu.VMEM((X, CORES, Y, ROWS, ROWS), f32),
        pltpu.VMEM((Y * ROWS, depth), bf16),
        pltpu.VMEM((Y * ROWS, depth), bf16),
        pltpu.VMEM((CHUNKS, Z, ROWS, BLOCK), f32),
        pltpu.VMEM((len(WAVES), depth, 2 * BLOCK), bf16),
        pltpu.VMEM((len(WAVES), depth, 2 * BLOCK), bf16),
        pltpu.VMEM((len(EARLY), Y - 1, ROWS, BLOCK), f32),
        pltpu.VMEM((2, Y, ROWS, 2 * BLOCK), f32),
        pltpu.VMEM((GROUPS, 2 * BLOCK, BLOCK), f32),
        pltpu.VMEM((GROUPS, Y - 1, 2 * BLOCK // Y, BLOCK), f32),
        pltpu.VMEM((GROUPS, 2 * BLOCK // Y, BLOCK), f32),
        pltpu.VMEM((GROUPS, Z - 1, 2 * BLOCK // Y // Z, BLOCK), f32),
        pltpu.VMEM((GROUPS, Y, 2 * BLOCK // Y, BLOCK), f32),
        pltpu.SemaphoreType.DMA((count,)),
        pltpu.SemaphoreType.DMA((count,)),
        pltpu.SemaphoreType.DMA((2,)),
        pltpu.SemaphoreType.DMA((len(WAVES) + GROUPS,)),
    ]
    for wave in WAVES:
        width = len(wave) * BLOCK
        scratch += [
            pltpu.VMEM((Y, ROWS, width), f32),
            pltpu.VMEM((2, ROWS // 2, width), f32),
            pltpu.VMEM((2, ROWS // 2, width), f32),
            pltpu.VMEM((2, ROWS, width), f32),
        ]
    anywhere = pl.BlockSpec(memory_space=pl.ANY)
    product, terms = pl.pallas_call(
        functools.partial(kernel, order),
        out_shape=(
            jax.ShapeDtypeStruct(panels.shape, f32),
            jax.ShapeDtypeStruct((GROUPS, Y, 2 * BLOCK // Y, BLOCK), f32),
        ),
        in_specs=[anywhere, anywhere, pl.BlockSpec(memory_space=pltpu.SMEM)],
        out_specs=(anywhere, anywhere),
        scratch_shapes=scratch,
        compiler_params=pltpu.CompilerParams(
            collective_id=0, has_side_effects=True, vmem_limit_bytes=60 * 1024 * 1024
        ),
        cost_estimate=pl.CostEstimate(flops=2 * 8192**3 // 256, bytes_accessed=5 * 2**20, transcendentals=0),
        name="selected_inverse",
    )(top_inverse, panels, fill_pattern)
    return -product, diagonal_part + terms.reshape(diagonal_part.shape)


def solution(mesh):
    in_specs = (P("row", "col"), P("row", "col"), P("col", None), P("col", None))
    out_specs = (P("row", "col"), P("col", None))
    return jax.shard_map(local, mesh=mesh, in_specs=in_specs, out_specs=out_specs, check_vma=False)
```

```python
import functools

import jax
import jax.numpy as jnp
from jax import lax
from jax.experimental import pallas as pl
from jax.experimental.pallas import tpu as pltpu
from jax.sharding import PartitionSpec as P

BLOCK = 128
Z, Y, X, CORES = 8, 4, 4, 2
ROWS = 2 * BLOCK
CHUNKS = 8
WAVES = ((0, 1), (2, 3), (4,), (5,), (6,), (7,))
GROUPS = 4
EARLY = (4, 5, 6, 7)
TURNS = ((0, 1, 2, 3, 6, 4, 7, 5), (0, 1, 2, 3, 4, 5, 6, 7))
GATE = 1.500
LONG = (0, 1, 0, 1, 1, 1, 0, 0)
LINK = 96e3
HOP = 3.5


def steps(way, q):
    return 4 if LONG[q] == way else 3


def zslot(way, s):
    return s if way == 0 else (Z - s) % Z


def arrival_of(q, d):
    if d < 4 or (d == 4 and LONG[q] == 0):
        return ("z", 0, q, d - 1)
    return ("z", 1, q, Z - 1 - d)


def near_slots(q):
    return (5, 6, 7) if LONG[q] else (1, 2, 3)


def far_slots(q):
    return (1, 2, 3) if LONG[q] else (5, 6, 7)


class Plan:
    def __init__(self):
        self.tasks = []

    def add(self, name, rank, after=(), needs=(), sends=(), cost=0.0, gate=None):
        self.tasks.append(
            dict(name=name, rank=rank, after=after, needs=needs, sends=sends, cost=cost, gate=gate)
        )

    def order(self):
        now, free, arrived, done, result = 0.0, {}, {}, set(), []
        left = list(self.tasks)
        while left:
            best = None
            for task in left:
                if not all(n in done for n in task["after"]) or not all(n in arrived for n in task["needs"]):
                    continue
                ready = max([arrived[n] for n in task["needs"]], default=0.0)
                if task["gate"] is not None:
                    link, depth = task["gate"]
                    ready = max(ready, free.get(link, 0.0) - depth)
                ready = max(ready, now)
                key = (ready, task["rank"])
                if best is None or key < best[0]:
                    best = (key, task)
            (ready, _), task = best
            now = ready + task["cost"]
            for ident, link, size in task["sends"]:
                now += 0.09
                if link[0] == "far":
                    free[link[1]] = max(now, free.get(link[1], 0.0)) + size / LINK
                    arrived[ident] = max(now, free[link[1]]) + (4.0 if link[1][0] == "z" else 3.5)
                else:
                    rate = 6 * LINK if link == "s" else LINK
                    begin = max(now, free.get(link, 0.0))
                    free[link] = begin + size / rate
                    arrived[ident] = free[link] + HOP
                    task.setdefault("sent", []).append((ident, free[link]))
            done.add(task["name"])
            left.remove(task)
            result.append((ready, task))
        return result, now


def make_plan():
    plan = Plan()
    piece = ROWS * BLOCK * 4 * CORES
    for q in range(CHUNKS):
        plan.add(("mask", q), (1, q) if q else (0, 0), cost=0.15)
        for way in range(2):
            turn = TURNS[way].index(q)
            plan.add(
                ("zown", way, q), (0, 1, way) if q == 0 else (2, turn, way),
                after=[("mask", q)] + ([("zown", way, TURNS[way][turn - 1])] if turn else []),
                sends=[(("z", way, q, 0), ("z", way), piece)], gate=(("z", way), GATE),
            )
            for s in range(1, steps(way, q)):
                plan.add(
                    ("zfwd", way, q, s), (1, turn, s), needs=[("z", way, q, s - 1)],
                    sends=[(("z", way, q, s), ("z", way), piece)],
                )
    block = ROWS * ROWS * 4 * CORES
    plan.add(
        ("a2a",), (0, 2),
        sends=[(("a", 3), ("y", 0), block), (("a", 1), ("y", 1), block), (("a", 2), ("y", 0), 2 * block)],
    )
    plan.add(("acopy",), (0, 3), cost=0.15)
    for j in range(Y):
        plan.add(
            ("xown", j), (0, 4), after=[("acopy",)], needs=[("a", j)] if j else [],
            sends=[(("x", 1, j), ("x", 0), block), (("x", 3, j), ("x", 1), block), (("s", 0, j), "s", block // 2)],
        )
        for e in (1, 3):
            sends = [(("s", e, j), "s", block // 2)]
            if (e == 1) == (j in (0, 3)):
                sends.append((("x", 2, j), ("x", e // 2), block))
            plan.add(("xfwd", e, j), (0, 5), needs=[("x", e, j)], sends=sends)
        plan.add(("xfwd", 2, j), (0, 5), needs=[("x", 2, j)], sends=[(("s", 2, j), "s", block // 2)])
    for e in range(X):
        for k in range(CORES):
            needs = [("s", e, j) if k else ("x", e, j) for j in range(Y)]
            if (e, k) == (0, 0):
                needs = [("a", j) for j in range(1, Y)]
            plan.add(("aconv", e, k), (3,), after=[("acopy",)], needs=needs, cost=0.5)
    for q in EARLY:
        plan.add(
            ("share", q), (6, q), after=[("mask", q)], gate=(("y", q % 2), 0.0),
            sends=[(("p", q, 3), ("y", 0), piece), (("p", q, 1), ("y", 1), piece)],
        )
        plan.add(
            ("relay", q), (6, q), needs=[("p", q, 1 if q % 2 else 3)],
            sends=[(("p", q, 2), ("y", q % 2), piece)],
        )
    for w, wave in enumerate(WAVES):
        width = len(wave) * BLOCK
        for d in range(Z):
            needs = [arrival_of(q, d) for q in wave] if d else []
            after = [("mask", q) for q in wave]
            plan.add(("pconv", w, d), (4, w), after=after, needs=needs, cost=0.15)
        half = ROWS // 2 * width * 4 * CORES
        after = [("aconv", e, k) for e in range(X) for k in range(CORES)]
        early = wave[0] in EARLY
        for j in range(Y):
            before = after + [("pconv", w, d) for d in (0,) + near_slots(wave[0])]
            before += [("early", w - 2)] if w >= 2 and WAVES[w - 2][0] in EARLY else []
            plan.add(("near", w, j), (5, w, j), after=before if early else [], cost=(0.2 + 0.15 * len(wave)) if early else 0.0)
            before = [("near", w, j), ("pconv", w, 4)]
            plan.add(("join", w, j), (2, w, j), after=before if early else [], cost=(0.1 + 0.05 * len(wave)) if early else 0.0)
        if early:
            plan.add(
                ("early", w), (2, 2), after=[("join", w, j) for j in range(Y)],
                needs=[("p", q, j) for q in wave for j in range(1, Y)], cost=0.7 * len(wave),
            )
        after += [("pconv", w, d) for d in range(Z)] + [("join", w, j) for j in range(Y)]
        for j, sends in (
            (2, [(("r1", w, 0), ("y", 0), half), (("r1", w, 1), ("y", 1), half)]),
            (1, [(("r2", w, 0, 1), ("y", 0), half)]),
            (3, [(("r2", w, 1, 0), ("y", 1), half)]),
            (0, []),
        ):
            plan.add(("mm", w, j), (5, w, (2, 1, 3, 0).index(j)), after=after, sends=sends, cost=(0.2 + 0.1 * len(wave)) if early else 0.75)
        for way in range(2):
            plan.add(
                ("radd", w, way), (2, 0), after=[("mm", w, 1 + 2 * way)], needs=[("r1", w, way)],
                sends=[(("r2", w, way, way), ("y", way), half)], cost=0.1,
            )
        plan.add(
            ("fin", w), (2, 1), after=[("mm", w, 0), ("radd", w, 0), ("radd", w, 1)],
            needs=[("r2", w, way, h) for way in range(2) for h in range(2)], cost=0.8,
        )
    small = 2 * BLOCK // Y * BLOCK * 4 * CORES
    for g in range(GROUPS):
        stage = "early" if 2 * g in EARLY else "fin"
        owners = [(stage, w) for w, wave in enumerate(WAVES) if set(wave) & {2 * g, 2 * g + 1}]
        plan.add(("d1", g), (2, 2), after=owners, sends=[(("d1", g, j), ("far", ("y", j // 2)), small * min(j, Y - j)) for j in (2, 1, 3)])
        plan.add(
            ("d2", g), (2, 2), needs=[("d1", g, j) for j in range(1, Y)],
            sends=[(("d2", g, i), ("far", ("z", i // 4)), small // Z * min(i, Z - i)) for i in (4, 3, 5, 2, 6, 1, 7)], cost=0.1,
        )
        plan.add(
            ("d3", g), (2, 2), needs=[("d2", g, i) for i in range(1, Z)],
            sends=[(("d3", g, i), ("far", ("z", i // 4)), small // Z * min(i, Z - i)) for i in (4, 3, 5, 2, 6, 1, 7)], cost=0.1,
        )
        plan.add(
            ("d4", g), (2, 2), needs=[("d3", g, i) for i in range(1, Z)],
            sends=[(("d4", g, j), ("far", ("y", j // 2)), small * min(j, Y - j)) for j in range(1, Y)],
        )
        plan.add(("d5", g), (2, 2), needs=[("d4", g, j) for j in range(1, Y)], cost=0.1)
    return plan


def split(v):
    high = v.astype(jnp.bfloat16)
    return high, (v - high.astype(jnp.float32)).astype(jnp.bfloat16)


def outer(a, b):
    return lax.dot_general(
        a, b, (((0,), (0,)), ((), ())), precision=lax.Precision.HIGHEST, preferred_element_type=jnp.float32
    )


def dot(a, b):
    return jnp.dot(a, b, preferred_element_type=jnp.float32)


def kernel(order, a_any, p_any, fill_ref, x_any, g_any, a_ref, p_ref, x_ref, *scratch):
    (agat, ahi, alo, pgat, phi, plo, py, yh, t, dr1, s1, dr2, res, send_sem, recv_sem, in_sem, out_sem) = scratch[:17]
    waves = scratch[17:]
    xp, xr1, xs, xr2 = waves[0::4], waves[1::4], waves[2::4], waves[3::4]
    r, c = lax.axis_index("row"), lax.axis_index("col")
    z, y, x, core = lax.div(r, Y), lax.rem(r, Y), lax.div(c, CORES), lax.rem(c, CORES)

    def device(dz=0, dy=0, dx=0, dc=0):
        return {
            "row": lax.rem(z + dz, Z) * Y + lax.rem(y + dy, Y),
            "col": lax.rem(x + dx, X) * CORES + lax.rem(core + dc, CORES),
        }

    def part(index, size):
        return pl.ds(pl.multiple_of(index * size, size), size)

    partners = [device(dz=i) for i in range(1, Z)] + [device(dy=j) for j in range(1, Y)]
    partners += [device(dx=1), device(dx=X - 1), device(dc=1)]
    barrier = pltpu.get_barrier_semaphore()
    for partner in partners:
        pl.semaphore_signal(barrier, inc=1, device_id=partner, device_id_type=pl.DeviceIdType.MESH)
    inputs = [pltpu.make_async_copy(p_any, p_ref, in_sem.at[0]), pltpu.make_async_copy(a_any, a_ref, in_sem.at[1])]
    for copy in inputs:
        copy.start()
    outputs = []

    def write(source, target):
        copy = pltpu.make_async_copy(source, target, out_sem.at[len(outputs)])
        copy.start()
        outputs.append(copy)

    half, quarter, eighth = ROWS // 2, 2 * BLOCK // Y, 2 * BLOCK // Y // Z

    def ends(ident):
        kind, *at = ident
        if kind == "z":
            way, q, s = at
            return (
                pgat.at[q, zslot(way, s)], pgat.at[q, zslot(way, s + 1)],
                device(dz=1 if way == 0 else Z - 1),
            )
        if kind == "a":
            (j,) = at
            i = Y - j
            return a_ref.at[:, part(lax.rem(y + i, Y), ROWS)], agat.at[0, 0, j], device(dy=i)
        if kind == "x":
            e, j = at
            if e == 2:
                way = 0 if j in (0, 3) else 1
                source = agat.at[1 + 2 * way, 0, j]
            else:
                way, source = e // 2, agat.at[0, 0, j]
            return source, agat.at[e, 0, j], device(dx=1 if way == 0 else X - 1)
        if kind == "s":
            e, j = at
            return agat.at[e, 0, j], agat.at[e, 1, j], device(dc=1)
        if kind == "p":
            q, j = at
            source, where = pgat.at[q, 0], device(dy=Y - j)
            if j == 2:
                source = py.at[q - EARLY[0], 0 if q % 2 else 2]
                where = device(dy=Y - 1 if q % 2 else 1)
            return source, py.at[q - EARLY[0], j - 1], where
        if kind == "r1":
            w, way = at
            return xp[w].at[2, pl.ds(way * half, half)], xr1[w].at[way], device(dy=1 if way == 0 else Y - 1)
        if kind == "r2":
            w, way, h = at
            rows = pl.ds(h * half, half)
            source = xs[w].at[way] if h == way else xp[w].at[1 + 2 * way, rows]
            return source, xr2[w].at[way, rows], device(dy=1 if way == 0 else Y - 1)
        if kind == "d1":
            g, j = at
            return t.at[g, part(lax.rem(y + j, Y), quarter)], dr1.at[g, j - 1], device(dy=j)
        if kind == "d2":
            g, i = at
            return s1.at[g, part(lax.rem(z + i, Z), eighth)], dr2.at[g, i - 1], device(dz=i)
        if kind == "d3":
            g, i = at
            where = res.at[g, y, part(z, eighth)]
            return where, where, device(dz=i)
        g, j = at
        return res.at[g, y], res.at[g, y], device(dy=j)

    def fill(q, i):
        return fill_ref[q, 2 * r + i].astype(jnp.float32)

    def product(w, j, slot, count):
        cols = slice(0, len(WAVES[w]) * BLOCK)
        rows, depth = slice(j * ROWS, (j + 1) * ROWS), slice(slot * ROWS, (slot + count) * ROWS)
        high, low = phi[w, depth, cols], plo[w, depth, cols]
        return dot(ahi[rows, depth], high) + dot(ahi[rows, depth], low) + dot(alo[rows, depth], high)

    def body(name):
        kind, *at = name
        if kind == "mask":
            (q,) = at
            for i in range(2):
                rows = slice(i * BLOCK, (i + 1) * BLOCK)
                pgat[q, 0, rows] = p_ref[rows, q * BLOCK : (q + 1) * BLOCK] * fill(q, i)
        elif kind == "acopy":
            agat[0, 0, 0] = a_ref[:, part(y, ROWS)]
        elif kind == "aconv":
            e, k = at
            owner = lax.rem(x + X - e, X) * CORES + lax.rem(core + k, CORES)
            place = part(lax.rem(z + Z - owner, Z), ROWS)

            @pl.loop(0, Y)
            def _(j):
                high, low = split(agat[e, k, j])
                ahi[part(j, ROWS), place] = high
                alo[part(j, ROWS), place] = low

        elif kind == "pconv":
            w, d = at
            for i, q in enumerate(WAVES[w]):
                high, low = split(pgat[q, d])
                phi[w, d * ROWS : (d + 1) * ROWS, i * BLOCK : (i + 1) * BLOCK] = high
                plo[w, d * ROWS : (d + 1) * ROWS, i * BLOCK : (i + 1) * BLOCK] = low
        elif kind == "mm":
            w, j = at
            if WAVES[w][0] in EARLY:
                xp[w][j] += product(w, j, far_slots(WAVES[w][0])[0], 3)
            else:
                xp[w][j] = product(w, j, 0, Z)
        elif kind == "near":
            w, j = at
            if WAVES[w][0] in EARLY:
                own = product(w, j, 0, 1)
                near = product(w, j, near_slots(WAVES[w][0])[0], 3)
                xp[w][j] = own + near
                yh[w % 2, j, :, : len(WAVES[w]) * BLOCK] = 0.5 * own + near
        elif kind == "join":
            w, j = at
            if WAVES[w][0] in EARLY:
                opposite = product(w, j, 4, 1)
                xp[w][j] += opposite
                yh[w % 2, j, :, : len(WAVES[w]) * BLOCK] += 0.5 * opposite
        elif kind == "radd":
            w, way = at
            rows = slice(way * half, (way + 1) * half)
            xs[w][way] = xp[w][1 + 2 * way, rows] + xr1[w][way]
        elif kind == "early":
            (w,) = at
            for n, q in enumerate(WAVES[w]):
                cols = slice(n * BLOCK, (n + 1) * BLOCK)
                total = outer(pgat[q, 0], yh[w % 2, 0, :, cols])
                for j in range(1, Y):
                    total += outer(py[q - EARLY[0], j - 1], yh[w % 2, j, :, cols])
                t[q // 2, q % 2 * BLOCK : (q % 2 + 1) * BLOCK] = total + total.T
        elif kind == "fin":
            (w,) = at
            total = xp[w][0] + xr2[w][0] + xr2[w][1]
            for n, q in enumerate(WAVES[w]):
                mine = total[:, n * BLOCK : (n + 1) * BLOCK]
                mine = jnp.concatenate([mine[i * BLOCK : (i + 1) * BLOCK] * fill(q, i) for i in range(2)], axis=0)
                x_ref[:, q * BLOCK : (q + 1) * BLOCK] = mine
                if q not in EARLY:
                    t[q // 2, q % 2 * BLOCK : (q % 2 + 1) * BLOCK] = outer(pgat[q, 0], mine)
            cols = slice(WAVES[w][0] * BLOCK, (WAVES[w][-1] + 1) * BLOCK)
            write(x_ref.at[:, cols], x_any.at[:, cols])
        elif kind == "d2":
            (g,) = at
            s1[g] = t[g, part(y, quarter)] + dr1[g, 0] + dr1[g, 1] + dr1[g, 2]
        elif kind == "d3":
            (g,) = at
            total = s1[g, part(z, eighth)]
            for i in range(Z - 1):
                total += dr2[g, i]
            res[g, y, part(z, eighth)] = total
        elif kind == "d5":
            (g,) = at
            write(res.at[g], g_any.at[g])

    copies = {}
    waited = set()
    sent = []
    for now, task in order:
        while sent and sent[0][0] < now - 3.0:
            copies[sent.pop(0)[1]].wait_send()
        if task["name"] == ("mask", 0):
            inputs[0].wait()
        if task["name"] == ("a2a",):
            inputs[1].wait()
        for ident in task["needs"]:
            if ident not in waited:
                waited.add(ident)
                copies[ident].wait_recv()
        body(task["name"])
        for ident, _, _ in task["sends"]:
            source, target, where = ends(ident)
            n = len(copies)
            if n == 0:
                pl.semaphore_wait(barrier, len(partners))
            copies[ident] = pltpu.make_async_remote_copy(
                src_ref=source, dst_ref=target, send_sem=send_sem.at[n], recv_sem=recv_sem.at[n],
                device_id=where, device_id_type=pl.DeviceIdType.MESH,
            )
            copies[ident].start()
            sent.append((now if ident[0][0] == "d" else dict(task["sent"])[ident], ident))
        sent.sort(key=lambda entry: entry[0])
    for _, ident in sent:
        copies[ident].wait_send()
    for ident, copy in copies.items():
        if ident not in waited:
            copy.wait_recv()
    for copy in outputs:
        copy.wait()


def local(top_inverse, panels, fill_pattern, diagonal_part):
    order, _ = make_plan().order()
    count = sum(len(task["sends"]) for _, task in order)
    f32, bf16 = jnp.float32, jnp.bfloat16
    depth = Z * ROWS
    scratch = [
        pltpu.VMEM((ROWS, Y * ROWS), f32),
        pltpu.VMEM((ROWS, CHUNKS * BLOCK), f32),
        pltpu.VMEM((ROWS, CHUNKS * BLOCK), f32),
        pltpu.VMEM((X, CORES, Y, ROWS, ROWS), f32),
        pltpu.VMEM((Y * ROWS, depth), bf16),
        pltpu.VMEM((Y * ROWS, depth), bf16),
        pltpu.VMEM((CHUNKS, Z, ROWS, BLOCK), f32),
        pltpu.VMEM((len(WAVES), depth, 2 * BLOCK), bf16),
        pltpu.VMEM((len(WAVES), depth, 2 * BLOCK), bf16),
        pltpu.VMEM((len(EARLY), Y - 1, ROWS, BLOCK), f32),
        pltpu.VMEM((2, Y, ROWS, 2 * BLOCK), f32),
        pltpu.VMEM((GROUPS, 2 * BLOCK, BLOCK), f32),
        pltpu.VMEM((GROUPS, Y - 1, 2 * BLOCK // Y, BLOCK), f32),
        pltpu.VMEM((GROUPS, 2 * BLOCK // Y, BLOCK), f32),
        pltpu.VMEM((GROUPS, Z - 1, 2 * BLOCK // Y // Z, BLOCK), f32),
        pltpu.VMEM((GROUPS, Y, 2 * BLOCK // Y, BLOCK), f32),
        pltpu.SemaphoreType.DMA((count,)),
        pltpu.SemaphoreType.DMA((count,)),
        pltpu.SemaphoreType.DMA((2,)),
        pltpu.SemaphoreType.DMA((len(WAVES) + GROUPS,)),
    ]
    for wave in WAVES:
        width = len(wave) * BLOCK
        scratch += [
            pltpu.VMEM((Y, ROWS, width), f32),
            pltpu.VMEM((2, ROWS // 2, width), f32),
            pltpu.VMEM((2, ROWS // 2, width), f32),
            pltpu.VMEM((2, ROWS, width), f32),
        ]
    anywhere = pl.BlockSpec(memory_space=pl.ANY)
    product, terms = pl.pallas_call(
        functools.partial(kernel, order),
        out_shape=(
            jax.ShapeDtypeStruct(panels.shape, f32),
            jax.ShapeDtypeStruct((GROUPS, Y, 2 * BLOCK // Y, BLOCK), f32),
        ),
        in_specs=[anywhere, anywhere, pl.BlockSpec(memory_space=pltpu.SMEM)],
        out_specs=(anywhere, anywhere),
        scratch_shapes=scratch,
        compiler_params=pltpu.CompilerParams(
            collective_id=0, has_side_effects=True, vmem_limit_bytes=60 * 1024 * 1024
        ),
        cost_estimate=pl.CostEstimate(flops=2 * 8192**3 // 256, bytes_accessed=5 * 2**20, transcendentals=0),
        name="selected_inverse",
    )(top_inverse, panels, fill_pattern)
    return -product, diagonal_part + terms.reshape(diagonal_part.shape)


def solution(mesh):
    in_specs = (P("row", "col"), P("row", "col"), P("col", None), P("col", None))
    out_specs = (P("row", "col"), P("col", None))
    return jax.shard_map(local, mesh=mesh, in_specs=in_specs, out_specs=out_specs, check_vma=False)
```
